32 devices in a mesh: lon: 4 (over y, x), lat: 8 (over z, core).
Axes of the slice: x: 2, y: 2, z: 4, core: 2. Of those that a mesh axis runs over, the one named last changes fastest.
Arguments:
- tracers: float32 [4, 16, 1024, 512], P(None, None, 'lat', 'lon'), may hold values from -6 to 6
- fill_fraction: float32 [16, 1024, 512], P(None, 'lat', 'lon'), may hold values from 0.3 to 1
- ocean_mask: int32 [16, 1024, 512], P(None, 'lat', 'lon'), may hold values 0 or 1
- east_speed: float32 [16, 1024, 512], P(None, 'lat', 'lon'), may hold values from -3 to 3
- north_speed: float32 [16, 1024, 512], P(None, 'lat', 'lon'), may hold values from -3 to 3
- diffusivity: float32 [16], replicated, may hold values from 0.1 to 1
- cell_area: float32 [1024, 512], P('lat', 'lon'), may hold values from 0.25 to 1
- owner_map: int32 [4096, 1], P(('lon', 'lat')), may hold values from 0 to 31; in each aligned block of 128 rows (0 to 127, 128 to 255, ...) at most 8 rows name the same one
Outputs:
- updated: float32 [4, 16, 1024, 512], P(None, None, 'lat', 'lon')
- received_two: float32 [32, 256, 2048], P(('lon', 'lat'))
- received_four: float32 [32, 256, 512], P(('lon', 'lat'))
The draws below stay inside these ranges and needn't reach their ends.
Inputs may be any that keep to these rules, and one draw needn't show every extreme that they name: `owner_map`: owner device numbers in lon-major order. Of the 128 rows of one device, at most 8 name the same owner, and in some device exactly 8 do.
All inputs are finite; a program needn't handle non-finite values. No bound on the sum of `ocean_mask` on one device may be relied on, other than what follows from the above.
Results may differ from the reference program's by a relative error of at most 0.00007.
Values sent between devices are 32-bit elements; how exact they have to be, the bound alone decides.
A program may use at most 128 MiB of HBM per device.

```python
import math
import jax
import jax.numpy as jnp
import numpy as np

TRACERS = 4
LEVELS = 16
BAND_ROWS = 16
NLON = 512
NLAT = 1024
UNITS = 128
CAP = 8
N_LON = 4
N_LAT = 8
DEVICES = 32


def with_ends(result, key, smallest, high):
    index_at = [jax.random.randint(jax.random.fold_in(key, axis), (), 0, length) for axis, length in enumerate(result.shape)]
    longest = result.shape.index(max(result.shape))
    next_to = index_at[:longest] + [(index_at[longest] + 1) % result.shape[longest]] + index_at[longest + 1:]
    return result.at[tuple(index_at)].set(smallest).at[tuple(next_to)].set(high)


def steps_of(own_key, shape, shards, least, largest):
    gain, own = 1.0, jax.random.fold_in(own_key, 6)
    for dim, shards_of in shards:
        steps = jnp.exp(jax.random.uniform(jax.random.fold_in(own, dim), (shards_of,), jnp.float32, least / len(shards), largest / len(shards)))
        gain = gain * jnp.repeat(steps, shape[dim] // shards_of).reshape([-1 if axis == dim else 1 for axis in range(len(shape))])
    return gain


def shared_out(key, own, number, rows, amount, top, bound, slope):
    ranking = jax.random.permutation(key, amount)
    crowded, common = portions_of(amount, rows * top, bound, slope, True), portions_of(amount, rows * top, bound, slope, False)
    places = jnp.arange(amount)

    def named(lengths, rotation):
        used = int((lengths > 0).sum())
        fixed = max(1, used // 4)
        shifted = fixed + (places - fixed + rotation * (used - fixed)) % max(1, amount - fixed)
        return jnp.zeros((amount,), jnp.int32).at[ranking[jnp.where(places < fixed, places, shifted)]].set(jnp.asarray(lengths, jnp.int32))

    lengths = jnp.where(number % 4 == 0, named(crowded, number // 4), named(common, number - number // 4 - 1))
    mixed = jax.random.permutation(jax.random.fold_in(own, 3), amount)
    source_of, taker = mixed[0:amount // 2 * 2:2], mixed[1:amount // 2 * 2:2]
    margin = jnp.minimum(lengths[source_of] - 1, bound - lengths[taker]) // 2
    margin = jnp.where((source_of == ranking[0]) | (taker == ranking[0]) | (lengths[taker] == 0), 0, jnp.maximum(margin, 0))
    shifted = jax.random.randint(jax.random.fold_in(own, 4), (amount // 2,), 0, 1 << 20) % (margin + 1)
    lengths = lengths.at[source_of].add(-shifted).at[taker].add(shifted)
    items = jnp.searchsorted(jnp.cumsum(lengths), jnp.arange(rows * top), side="right").astype(jnp.int32)
    listing = items.reshape(top, rows).T
    listing = listing[jax.random.permutation(jax.random.fold_in(own, 1), rows)]
    rotation = jax.random.randint(jax.random.fold_in(own, 2), (rows, 1), 0, top)
    return jnp.take_along_axis(listing, (jnp.arange(top)[None, :] + rotation) % top, axis=1)


def portions_of(count, total, bound, lean, full):
    weights = [(1 << 20) // math.isqrt(standing ** lean) + 1 for standing in range(1, count + 1)]
    largest = bound if full else min(bound, max(-(-total // count), total * weights[0] // sum(weights)))
    least = 1 if total - largest >= count - 1 else 0
    given, spare = [largest] + [least] * (count - 1), total - largest - least * (count - 1)
    while spare > 0:
        free = [i for i in range(1, count) if given[i] < largest] or [i for i in range(1, count) if given[i] < bound]
        mass, budget = sum([weights[i] for i in free]), spare
        for i in free:
            addition = min(bound - given[i], max(1, budget * weights[i] // mass), spare)
            given[i] = given[i] + addition
            spare = spare - addition
    return np.array(given)


def bell_draw(key, shape, deviation, reach, cuts=(), held_as=jnp.bfloat16):
    gain = steps_of(key, shape, cuts, -0.22, 0.18) if cuts else 1.0
    result = jax.random.normal(key, shape, jnp.float32) * deviation * gain
    return jnp.minimum(jnp.maximum(result, -reach), reach).astype(held_as)


def setup_inputs(seed: int = 0) -> dict:
    splits = jax.random.split(jax.random.key(seed), 9)
    tracers = bell_draw(splits[0], (TRACERS, LEVELS, NLAT, NLON), 1.0, 6.0, ((2, 8), (3, 4)), jnp.float32)
    fill_fraction = jnp.clip(jnp.exp(math.log(1.0) - 1.2039728 * jax.random.uniform(splits[1], (LEVELS, NLAT, NLON), jnp.float32) ** steps_of(splits[1], (LEVELS, NLAT, NLON), ((1, 8), (2, 4)), -0.2, 0.2)), 0.3, 1.0)
    ocean_mask = with_ends((jax.random.randint(splits[2], (LEVELS, NLAT, NLON), 0, 2) < 1).astype(jnp.int32), jax.random.fold_in(splits[2], 1), 0, 1)
    east_speed = bell_draw(splits[3], (LEVELS, NLAT, NLON), 0.5, 3.0, ((1, 8), (2, 4)), jnp.float32)
    north_speed = bell_draw(splits[4], (LEVELS, NLAT, NLON), 0.5, 3.0, ((1, 8), (2, 4)), jnp.float32)
    diffusivity = jnp.clip(jnp.exp(jax.random.uniform(splits[5], (LEVELS,), jnp.float32, math.log(0.1), math.log(1.0))), 0.1, 1.0)
    cell_area = jnp.clip(jnp.exp(math.log(1.0) - 1.3862944 * jax.random.uniform(splits[6], (NLAT, NLON), jnp.float32) ** steps_of(splits[6], (NLAT, NLON), ((0, 8), (1, 4)), -0.2, 0.2)), 0.25, 1.0)
    owner_map_keys = jax.random.split(jax.random.fold_in(splits[7], 1), (DEVICES * UNITS) // UNITS)
    owner_map_turns = jax.random.permutation(jax.random.fold_in(splits[7], 3), (DEVICES * UNITS) // UNITS)
    owner_map = jax.vmap(lambda own, number: shared_out(jax.random.fold_in(splits[7], 2), own, number, UNITS, DEVICES, 1, CAP, 2))(owner_map_keys, owner_map_turns).reshape((DEVICES * UNITS, 1))
    return dict(tracers=tracers, fill_fraction=fill_fraction, ocean_mask=ocean_mask, east_speed=east_speed, north_speed=north_speed, diffusivity=diffusivity, cell_area=cell_area, owner_map=owner_map)


time_step = 0.05
depth_floor = 0.25
weight_floor = 0.25


def face_flux(lower_val, upper_val, lower_h, upper_h, lower_speed, upper_speed, mixing):
    open_depth = jnp.minimum(lower_h, upper_h)
    face_speed = 0.5 * (lower_speed + upper_speed)
    return open_depth * (0.5 * face_speed * (lower_val + upper_val) - 0.5 * jnp.abs(face_speed) * (upper_val - lower_val) - mixing * (upper_val - lower_val))


def pool_pairs(field):
    old_shape = field.shape
    return field.reshape(old_shape[:-2] + (old_shape[-2] // 2, 2, old_shape[-1] // 2, 2)).sum(axis=(-3, -1))


def coarsen(updated, weight):
    weighted = pool_pairs(updated * weight[None])
    weight_two = pool_pairs(weight)
    weighted_four = pool_pairs(weighted)
    weight_four = pool_pairs(weight_two)
    coarse_two = weighted / jnp.maximum(weight_two, weight_floor)[None]
    coarse_four = weighted_four / jnp.maximum(weight_four, weight_floor)[None]
    return coarse_two, coarse_four


def device_blocks(field, band):
    shape_of = field.shape
    bands = shape_of[2] // N_LAT // band
    width = shape_of[3] // N_LON
    split = field.reshape(shape_of[0], shape_of[1], N_LAT, bands, band, N_LON, width)
    moved = split.transpose(5, 2, 1, 3, 0, 4, 6)
    return moved.reshape(N_LON * N_LAT, shape_of[1] * bands, shape_of[0] * band * width)


def deliver(blocks, owners):
    devices = N_LON * N_LAT
    onehot = (owners[:, :, None] == jnp.arange(devices, dtype=jnp.int32)[None, None, :]).astype(jnp.int32)
    rank_in = jnp.sum((jnp.cumsum(onehot, axis=1) - onehot) * onehot, axis=2)
    slot_index = (owners * CAP + rank_in).astype(jnp.int32)
    source_ids = jnp.broadcast_to(jnp.arange(devices, dtype=jnp.int32)[:, None], slot_index.shape)
    width = blocks.shape[-1]
    buffers = jnp.zeros((devices, devices * CAP, width), jnp.float32).at[source_ids, slot_index].set(blocks)
    return buffers.reshape(devices, devices, CAP, width).transpose(1, 0, 2, 3).reshape(devices, devices * CAP, width)


def reference(tracers, fill_fraction, ocean_mask, east_speed, north_speed, diffusivity, cell_area, owner_map):
    wet_depth = fill_fraction * ocean_mask.astype(jnp.float32)
    mixing = diffusivity[:, None, None]
    h_east = jnp.roll(wet_depth, -1, axis=-1)
    u_east = jnp.roll(east_speed, -1, axis=-1)
    h_north = jnp.concatenate([wet_depth[:, 1:], jnp.flip(wet_depth[:, -1:], -1)], axis=1)
    v_north = jnp.concatenate([north_speed[:, 1:], -jnp.flip(north_speed[:, -1:], -1)], axis=1)
    volume = cell_area[None] * jnp.maximum(wet_depth, depth_floor)
    results = []
    for tracer_index in range(TRACERS):
        tracer = tracers[tracer_index]
        east_flux = face_flux(tracer, jnp.roll(tracer, -1, axis=-1), wet_depth, h_east, east_speed, u_east, mixing)
        west_flux = jnp.roll(east_flux, 1, axis=-1)
        north_val = jnp.concatenate([tracer[:, 1:], jnp.flip(tracer[:, -1:], -1)], axis=1)
        north_flux = face_flux(tracer, north_val, wet_depth, h_north, north_speed, v_north, mixing)
        south_flux = jnp.concatenate([jnp.zeros_like(north_flux[:, :1]), north_flux[:, :-1]], axis=1)
        results.append(tracer + time_step * ((west_flux - east_flux) + (south_flux - north_flux)) / volume)
    updated = jnp.stack(results, axis=0)
    coarse_two, coarse_four = coarsen(updated, cell_area[None] * wet_depth)
    owners = owner_map.reshape(N_LON * N_LAT, -1)
    received_two = deliver(device_blocks(coarse_two, BAND_ROWS // 2), owners)
    received_four = deliver(device_blocks(coarse_four, BAND_ROWS // 4), owners)
    return updated, received_two, received_four
```

```python
import functools

import jax
import jax.numpy as jnp
from jax import lax
from jax.experimental import pallas as pl
from jax.experimental.pallas import tpu as pltpu
from jax.sharding import PartitionSpec as P

BAND_ROWS = 16
MESH = pl.DeviceIdType.MESH

time_step = 0.05
depth_floor = 0.25
weight_floor = 0.25


def pieces(x):
    high = x.astype(jnp.bfloat16)
    rest = x - high.astype(jnp.float32)
    middle = rest.astype(jnp.bfloat16)
    low = (rest - middle.astype(jnp.float32)).astype(jnp.bfloat16)
    return high, middle, low


def dot(a, b):
    return jnp.dot(a, b, preferred_element_type=jnp.float32)


def exact_dot(x, ones):
    high, middle, low = pieces(x)
    return (dot(low, ones) + dot(middle, ones)) + dot(high, ones)


def kernel(
    sizes,
    tracers,
    fill,
    mask,
    east,
    north,
    mixing,
    area,
    owner,
    updated_out,
    recv_out,
    updated,
    depth,
    product,
    blocks,
    send,
    pool_two,
    pool_four,
    col_pack,
    col_got,
    row_pack,
    row_got,
    halo_send,
    halo_recv,
    send_sem,
    recv_sem,
    out_sem,
):
    n_lon, n_lat, rows_each = sizes
    n = n_lon * n_lat
    nt, nl, nr, nc = tracers.shape
    lon = lax.axis_index("lon")
    lat = lax.axis_index("lat")
    me = lon * n_lat + lat

    barrier = pltpu.get_barrier_semaphore()

    def greet(j, carry):
        target = lax.rem(me + j, n)
        pl.semaphore_signal(
            barrier, inc=1, device_id=(target // n_lat, lax.rem(target, n_lat)), device_id_type=MESH
        )
        return carry

    lax.fori_loop(1, n, greet, 0)

    lane = lax.broadcasted_iota(jnp.int32, (nr, nc), 1)
    row = lax.broadcasted_iota(jnp.int32, (nr, nc), 0)

    def pack(k, carry):
        west, east_side = carry
        depth[k] = fill[k] * mask[k].astype(jnp.float32)
        for item in range(nt + 2):
            if item < nt:
                x = tracers[item, k]
            elif item == nt:
                x = depth[k]
            else:
                x = east[k]
            at = item * nl + k
            west = jnp.where(lane == at, x[:, 0:1], west)
            east_side = jnp.where(lane == at, x[:, nc - 1 : nc], east_side)
            y = north[k] if item == nt + 1 else x
            row_pack[0, pl.ds(at, 1), :] = y[0:1, :]
            row_pack[1, pl.ds(at, 1), :] = y[nr - 1 : nr, :]
        return west, east_side

    zero = jnp.zeros((nr, nc), jnp.float32)
    west, east_side = lax.fori_loop(0, nl, pack, (zero, zero))
    col_pack[0] = west
    col_pack[1] = east_side

    at_fold = lat == n_lat - 1
    items = row_pack.shape[1]

    @pl.when(at_fold)
    def _():
        flip = (
            lax.broadcasted_iota(jnp.int32, (nc, nc), 0)
            + lax.broadcasted_iota(jnp.int32, (nc, nc), 1)
            == nc - 1
        )
        turned = exact_dot(row_pack[1], flip.astype(jnp.float32).astype(jnp.bfloat16))
        index = lax.broadcasted_iota(jnp.int32, (items, nc), 0)
        row_pack[1] = jnp.where(index >= (nt + 1) * nl, -turned, turned)

    @pl.when(lat == 0)
    def _():
        row_got[0] = jnp.zeros((items, nc), jnp.float32)

    pl.semaphore_wait(barrier, n - 1)

    def halo(src, dst, at_send, at_recv, to_lon, to_lat):
        return pltpu.make_async_remote_copy(
            src_ref=src,
            dst_ref=dst,
            send_sem=halo_send.at[at_send],
            recv_sem=halo_recv.at[at_recv],
            device_id=(to_lon, to_lat),
            device_id_type=MESH,
        )

    lon_west = lax.rem(lon + n_lon - 1, n_lon)
    lon_east = lax.rem(lon + 1, n_lon)
    to_west = halo(col_pack.at[0], col_got.at[1], 0, 1, lon_west, lat)
    to_east = halo(col_pack.at[1], col_got.at[0], 1, 0, lon_east, lat)
    to_south = halo(row_pack.at[0], row_got.at[1], 2, 3, lon, lat - 1)
    to_north = halo(row_pack.at[1], row_got.at[0], 3, 2, lon, lat + 1)
    to_fold = halo(row_pack.at[1], row_got.at[1], 3, 3, n_lon - 1 - lon, lat)
    to_west.start()
    to_east.start()

    @pl.when(lat > 0)
    def _():
        to_south.start()

    @pl.when(at_fold)
    def _():
        to_fold.start()

    @pl.when(jnp.logical_not(at_fold))
    def _():
        to_north.start()

    def matrix(shape, shift):
        hit = (lax.broadcasted_iota(jnp.int32, shape, 0) >> shift) == lax.broadcasted_iota(
            jnp.int32, shape, 1
        )
        return hit.astype(jnp.float32).astype(jnp.bfloat16)

    pool_two[...] = matrix(pool_two.shape, 1)
    pool_four[...] = matrix(pool_four.shape, 2)

    to_west.wait()
    to_east.wait()

    @pl.when(lat > 0)
    def _():
        to_south.wait_send()
        to_north.wait_recv()

    @pl.when(at_fold)
    def _():
        to_fold.wait()

    @pl.when(jnp.logical_not(at_fold))
    def _():
        to_north.wait_send()
        to_south.wait_recv()

    bands = nr // BAND_ROWS
    quads = BAND_ROWS // 4

    def level_out(k):
        return pltpu.make_async_copy(updated.at[:, k], updated_out.at[:, k], out_sem.at[k])

    def level(k, carry):
        def around(x, item):
            at = item * nl + k
            x_east = jnp.where(
                lane == nc - 1,
                pltpu.roll(col_got[1], nc - 1 - at, 1),
                pltpu.roll(x, nc - 1, 1),
            )
            x_west = jnp.where(
                lane == 0, pltpu.roll(col_got[0], nc - at, 1), pltpu.roll(x, 1, 1)
            )
            return x_east, x_west

        def along(x, item):
            at = item * nl + k
            x_north = jnp.where(
                row == nr - 1, row_got[1, pl.ds(at, 1), :], pltpu.roll(x, nr - 1, 0)
            )
            x_south = jnp.where(row == 0, row_got[0, pl.ds(at, 1), :], pltpu.roll(x, 1, 0))
            return x_north, x_south

        kappa = mixing[k]
        h = depth[k]
        u = east[k]
        v = north[k]
        grid_area = area[...]
        gain = time_step / (grid_area * jnp.maximum(h, depth_floor))
        h_east, h_west = around(h, nt)
        h_north, h_south = along(h, nt)
        u_east, u_west = around(u, nt + 1)
        v_north, v_south = along(v, nt + 1)

        def face(h_other, a, b):
            speed = 0.5 * (a + b)
            scaled = gain * jnp.minimum(h, h_other)
            return (
                scaled * (jnp.maximum(speed, 0.0) + kappa),
                scaled * (kappa - jnp.minimum(speed, 0.0)),
            )

        out_e, in_e = face(h_east, u, u_east)
        in_w, out_w = face(h_west, u_west, u)
        out_n, in_n = face(h_north, v, v_north)
        in_s, out_s = face(h_south, v_south, v)
        loss = (out_e + out_w) + (out_n + out_s)
        weight = grid_area * h
        product[nt] = weight
        for t in range(nt):
            x = tracers[t, k]
            x_east, x_west = around(x, t)
            x_north, x_south = along(x, t)
            change = (in_w * x_west + in_e * x_east) + (in_s * x_south + in_n * x_north)
            new = x + (change - loss * x)
            updated[t, k] = new
            product[t] = new * weight
        level_out(k).start()

        upper, lower, whole = [], [], []
        for t in range(nt + 1):
            both = []
            for i in range(quads):
                four = [
                    product[t, pl.ds(4 * i + j, bands, stride=BAND_ROWS), :] for j in range(4)
                ]
                upper.append(four[0] + four[1])
                lower.append(four[2] + four[3])
                both.append(upper[-1] + lower[-1])
            whole.append(jnp.concatenate(both, axis=1))
        two = exact_dot(
            jnp.concatenate(
                [jnp.concatenate(upper, axis=0), jnp.concatenate(lower, axis=0)], axis=1
            ),
            pool_two[...],
        )
        four = exact_dot(jnp.concatenate(whole, axis=0), pool_four[...])
        at_rows = pl.ds(pl.multiple_of(k * bands, bands), bands)
        span = quads * bands
        den_two = jnp.maximum(two[nt * span :], weight_floor)
        den_four = jnp.maximum(four[nt * bands :], weight_floor)
        for t in range(nt):
            ratio = two[t * span : (t + 1) * span] / den_two
            for i in range(quads):
                column = (t * quads + i) * nc
                blocks[at_rows, column : column + nc] = ratio[i * bands : (i + 1) * bands]
            column = (nt * quads + t) * nc
            blocks[at_rows, column : column + nc] = four[t * bands : (t + 1) * bands] / den_four
        return carry

    lax.fori_loop(0, nl, level, 0)

    units = blocks.shape[0]
    unit_a = lax.broadcasted_iota(jnp.int32, (units, units), 0)
    unit_b = lax.broadcasted_iota(jnp.int32, (units, units), 1)
    own_col = jnp.broadcast_to(owner[...], (units, units))
    own_row = jnp.sum(jnp.where(unit_a == unit_b, own_col, 0), axis=0, keepdims=True)
    earlier = jnp.logical_and(own_col == own_row, unit_a < unit_b)
    rank = jnp.sum(jnp.where(earlier, 1, 0), axis=0, keepdims=True)
    slot = own_row * rows_each + rank
    place = (
        (lax.broadcasted_iota(jnp.int32, (n * rows_each, units), 0) == slot)
        .astype(jnp.float32)
        .astype(jnp.bfloat16)
    )
    place = jnp.concatenate([place, place, place], axis=1)
    width = blocks.shape[1]
    chunk = 4 * nc
    for start in range(0, width, chunk):
        stop = min(width, start + chunk)
        send[:, start:stop] = dot(
            place, jnp.concatenate(pieces(blocks[:, start:stop]), axis=0)
        )

    mine = pl.ds(pl.multiple_of(me * rows_each, rows_each), rows_each)

    def to_peer(j):
        target = lax.rem(me + j, n)
        theirs = pl.ds(pl.multiple_of(target * rows_each, rows_each), rows_each)
        return pltpu.make_async_remote_copy(
            src_ref=send.at[theirs, :],
            dst_ref=recv_out.at[mine, :],
            send_sem=send_sem.at[j],
            recv_sem=recv_sem.at[j],
            device_id=(target // n_lat, lax.rem(target, n_lat)),
            device_id_type=MESH,
        )

    def begin(j, carry):
        to_peer(j).start()
        return carry

    lax.fori_loop(1, n, begin, 0)
    own_copy = pltpu.make_async_copy(send.at[mine, :], recv_out.at[mine, :], send_sem.at[0])
    own_copy.start()

    def end_level(k, carry):
        level_out(k).wait()
        return carry

    lax.fori_loop(0, nl, end_level, 0)
    own_copy.wait()

    def end(j, carry):
        source = lax.rem(me + n - j, n)
        theirs = pl.ds(pl.multiple_of(source * rows_each, rows_each), rows_each)
        copy = to_peer(j)
        copy.wait_send()
        pltpu.make_async_remote_copy(
            src_ref=send.at[mine, :],
            dst_ref=recv_out.at[theirs, :],
            send_sem=send_sem.at[j],
            recv_sem=recv_sem.at[j],
            device_id=(source // n_lat, lax.rem(source, n_lat)),
            device_id_type=MESH,
        ).wait_recv()
        return carry

    lax.fori_loop(1, n, end, 0)


def local(
    tracers, fill_fraction, ocean_mask, east_speed, north_speed, diffusivity, cell_area, owner_map
):
    nt, nl, nr, nc = tracers.shape
    n_lon = lax.axis_size("lon")
    n_lat = lax.axis_size("lat")
    n = n_lon * n_lat
    units = owner_map.shape[0]
    capacity = max(2, 2 * units // n)
    rows_each = -(-capacity // 8) * 8
    wide_two = nt * BAND_ROWS * nc // 4
    wide_four = nt * BAND_ROWS * nc // 16
    wide = wide_two + wide_four
    items = (nt + 2) * nl
    f32 = jnp.float32
    vmem = pl.BlockSpec(memory_space=pltpu.VMEM)
    updated, received = pl.pallas_call(
        functools.partial(kernel, (n_lon, n_lat, rows_each)),
        out_shape=(
            jax.ShapeDtypeStruct(tracers.shape, f32),
            jax.ShapeDtypeStruct((n * rows_each, wide), f32),
        ),
        in_specs=[vmem] * 5 + [pl.BlockSpec(memory_space=pltpu.SMEM)] + [vmem] * 2,
        out_specs=(pl.BlockSpec(memory_space=pl.ANY), pl.BlockSpec(memory_space=pl.ANY)),
        scratch_shapes=[
            pltpu.VMEM(tracers.shape, f32),
            pltpu.VMEM((nl, nr, nc), f32),
            pltpu.VMEM((nt + 1, nr, nc), f32),
            pltpu.VMEM((units, wide), f32),
            pltpu.VMEM((n * rows_each, wide), f32),
            pltpu.VMEM((2 * nc, nc), jnp.bfloat16),
            pltpu.VMEM((4 * nc, nc), jnp.bfloat16),
            pltpu.VMEM((2, nr, nc), f32),
            pltpu.VMEM((2, nr, nc), f32),
            pltpu.VMEM((2, items, nc), f32),
            pltpu.VMEM((2, items, nc), f32),
            pltpu.SemaphoreType.DMA((4,)),
            pltpu.SemaphoreType.DMA((4,)),
            pltpu.SemaphoreType.DMA((n,)),
            pltpu.SemaphoreType.DMA((n,)),
            pltpu.SemaphoreType.DMA((nl,)),
        ],
        compiler_params=pltpu.CompilerParams(
            collective_id=0, has_side_effects=True, vmem_limit_bytes=48 * 1024 * 1024
        ),
        name="substep",
    )(
        tracers,
        fill_fraction,
        ocean_mask,
        east_speed,
        north_speed,
        diffusivity,
        cell_area,
        owner_map,
    )
    if rows_each != capacity:
        received = received.reshape(n, rows_each, wide)[:, :capacity].reshape(n * capacity, wide)
    return updated, received[None, :, :wide_two], received[None, :, wide_two:]


def solution(mesh):
    in_specs = (
        P(None, None, "lat", "lon"),
        P(None, "lat", "lon"),
        P(None, "lat", "lon"),
        P(None, "lat", "lon"),
        P(None, "lat", "lon"),
        P(),
        P("lat", "lon"),
        P(("lon", "lat"), None),
    )
    out_specs = (
        P(None, None, "lat", "lon"),
        P(("lon", "lat"), None, None),
        P(("lon", "lat"), None, None),
    )
    return jax.shard_map(local, mesh=mesh, in_specs=in_specs, out_specs=out_specs, check_vma=False)
```

```python
import functools

import jax
import jax.numpy as jnp
from jax import lax
from jax.experimental import pallas as pl
from jax.experimental.pallas import tpu as pltpu
from jax.sharding import PartitionSpec as P

BAND_ROWS = 16
MESH = pl.DeviceIdType.MESH

time_step = 0.05
depth_floor = 0.25
weight_floor = 0.25


def pieces(x):
    high = x.astype(jnp.bfloat16)
    rest = x - high.astype(jnp.float32)
    middle = rest.astype(jnp.bfloat16)
    low = (rest - middle.astype(jnp.float32)).astype(jnp.bfloat16)
    return high, middle, low


def dot(a, b):
    return jnp.dot(a, b, preferred_element_type=jnp.float32)


def exact_dot(x, ones):
    high, middle, low = pieces(x)
    return (dot(low, ones) + dot(middle, ones)) + dot(high, ones)


def kernel(
    sizes,
    tracers_in,
    fill_in,
    mask_in,
    east_in,
    north_in,
    mixing,
    area_in,
    owner_in,
    updated_out,
    two_out,
    four_out,
    tracers,
    depth,
    mask,
    east,
    north,
    area,
    owner,
    updated,
    coef,
    product,
    den_two,
    den_four,
    blocks,
    send_first,
    send_rest,
    send_four,
    place,
    pool_two,
    pool_four,
    col_pack,
    col_got,
    row_pack,
    row_got,
    halo_send,
    halo_recv,
    send_sem,
    recv_sem,
    out_sem,
    in_sem,
):
    n_lon, n_lat, rows_each = sizes
    n = n_lon * n_lat
    nt, nl, nr, nc = tracers.shape
    lon = lax.axis_index("lon")
    lat = lax.axis_index("lat")
    me = lon * n_lat + lat

    barrier = pltpu.get_barrier_semaphore()
    inputs = [
        pltpu.make_async_copy(source, held, in_sem.at[index])
        for index, (source, held) in enumerate(
            (
                (fill_in, depth),
                (mask_in, mask),
                (east_in, east),
                (north_in, north),
                (tracers_in, tracers),
                (owner_in, owner),
                (area_in, area),
            )
        )
    ]
    for copy in inputs:
        copy.start()

    def greet(j, carry):
        target = lax.rem(me + j, n)
        pl.semaphore_signal(
            barrier, inc=1, device_id=(target // n_lat, lax.rem(target, n_lat)), device_id_type=MESH
        )
        return carry

    lax.fori_loop(1, n, greet, 0)

    lane = lax.broadcasted_iota(jnp.int32, (nr, nc), 1)
    row = lax.broadcasted_iota(jnp.int32, (nr, nc), 0)

    for copy in inputs:
        copy.wait()

    def pack(k, carry):
        west, east_side = carry
        depth[k] = depth[k] * mask[k].astype(jnp.float32)
        for item in range(nt + 2):
            if item < nt:
                x = tracers[item, k]
            elif item == nt:
                x = depth[k]
            else:
                x = east[k]
            at = item * nl + k
            west = jnp.where(lane == at, x[:, 0:1], west)
            east_side = jnp.where(lane == at, x[:, nc - 1 : nc], east_side)
            y = north[k] if item == nt + 1 else x
            row_pack[0, pl.ds(at, 1), :] = y[0:1, :]
            row_pack[1, pl.ds(at, 1), :] = y[nr - 1 : nr, :]
        return west, east_side

    zero = jnp.zeros((nr, nc), jnp.float32)
    west, east_side = lax.fori_loop(0, nl, pack, (zero, zero))
    col_pack[0] = west
    col_pack[1] = east_side

    at_fold = lat == n_lat - 1
    items = row_pack.shape[1]

    @pl.when(at_fold)
    def _():
        flip = (
            lax.broadcasted_iota(jnp.int32, (nc, nc), 0)
            + lax.broadcasted_iota(jnp.int32, (nc, nc), 1)
            == nc - 1
        )
        turned = exact_dot(row_pack[1], flip.astype(jnp.float32).astype(jnp.bfloat16))
        index = lax.broadcasted_iota(jnp.int32, (items, nc), 0)
        row_pack[1] = jnp.where(index >= (nt + 1) * nl, -turned, turned)

    @pl.when(lat == 0)
    def _():
        row_got[0] = jnp.zeros((items, nc), jnp.float32)

    pl.semaphore_wait(barrier, n - 1)

    def halo(src, dst, at_send, at_recv, to_lon, to_lat):
        return pltpu.make_async_remote_copy(
            src_ref=src,
            dst_ref=dst,
            send_sem=halo_send.at[at_send],
            recv_sem=halo_recv.at[at_recv],
            device_id=(to_lon, to_lat),
            device_id_type=MESH,
        )

    lon_west = lax.rem(lon + n_lon - 1, n_lon)
    lon_east = lax.rem(lon + 1, n_lon)
    to_west = halo(col_pack.at[0], col_got.at[1], 0, 1, lon_west, lat)
    to_east = halo(col_pack.at[1], col_got.at[0], 1, 0, lon_east, lat)
    to_south = halo(row_pack.at[0], row_got.at[1], 2, 3, lon, lat - 1)
    to_north = halo(row_pack.at[1], row_got.at[0], 3, 2, lon, lat + 1)
    to_fold = halo(row_pack.at[1], row_got.at[1], 3, 3, n_lon - 1 - lon, lat)
    to_west.start()
    to_east.start()

    @pl.when(lat > 0)
    def _():
        to_south.start()

    @pl.when(at_fold)
    def _():
        to_fold.start()

    @pl.when(jnp.logical_not(at_fold))
    def _():
        to_north.start()

    def matrix(shape, shift):
        hit = (lax.broadcasted_iota(jnp.int32, shape, 0) >> shift) == lax.broadcasted_iota(
            jnp.int32, shape, 1
        )
        return hit.astype(jnp.float32).astype(jnp.bfloat16)

    pool_two[...] = matrix(pool_two.shape, 1)
    pool_four[...] = matrix(pool_four.shape, 2)

    units = blocks.shape[0]
    unit_a = lax.broadcasted_iota(jnp.int32, (units, units), 0)
    unit_b = lax.broadcasted_iota(jnp.int32, (units, units), 1)
    own_row = owner[...]
    own_wide = jnp.broadcast_to(own_row, (units, units))
    own_col = jnp.sum(jnp.where(unit_a == unit_b, own_wide, 0), axis=1, keepdims=True)
    earlier = jnp.logical_and(own_col == own_wide, unit_a < unit_b)
    rank = jnp.sum(jnp.where(earlier, 1, 0), axis=0, keepdims=True)
    slot = own_row * rows_each + rank
    hit = (
        (lax.broadcasted_iota(jnp.int32, (n * rows_each, units), 0) == slot)
        .astype(jnp.float32)
        .astype(jnp.bfloat16)
    )
    place[...] = jnp.concatenate([hit, hit, hit], axis=1)

    to_west.wait()
    to_east.wait()

    @pl.when(lat > 0)
    def _():
        to_south.wait_send()
        to_north.wait_recv()

    @pl.when(at_fold)
    def _():
        to_fold.wait()

    @pl.when(jnp.logical_not(at_fold))
    def _():
        to_north.wait_send()
        to_south.wait_recv()

    bands = nr // BAND_ROWS
    quads = BAND_ROWS // 4

    def level_out(k):
        return pltpu.make_async_copy(updated.at[:, k], updated_out.at[:, k], out_sem.at[k])

    span = quads * bands

    def around(x, item, k):
        at = item * nl + k
        x_east = jnp.where(
            lane == nc - 1, pltpu.roll(col_got[1], nc - 1 - at, 1), pltpu.roll(x, nc - 1, 1)
        )
        x_west = jnp.where(lane == 0, pltpu.roll(col_got[0], nc - at, 1), pltpu.roll(x, 1, 1))
        return x_east, x_west

    def along(x, item, k):
        at = item * nl + k
        x_north = jnp.where(row == nr - 1, row_got[1, pl.ds(at, 1), :], pltpu.roll(x, nr - 1, 0))
        x_south = jnp.where(row == 0, row_got[0, pl.ds(at, 1), :], pltpu.roll(x, 1, 0))
        return x_north, x_south

    def faces(k):
        kappa = mixing[k]
        h = depth[k]
        u = east[k]
        v = north[k]
        grid_area = area[...]
        gain = time_step / (grid_area * jnp.maximum(h, depth_floor))
        h_east, h_west = around(h, nt, k)
        h_north, h_south = along(h, nt, k)
        u_east, u_west = around(u, nt + 1, k)
        v_north, v_south = along(v, nt + 1, k)

        def face(h_other, a, b):
            speed = 0.5 * (a + b)
            scaled = gain * jnp.minimum(h, h_other)
            return (
                scaled * (jnp.maximum(speed, 0.0) + kappa),
                scaled * (kappa - jnp.minimum(speed, 0.0)),
            )

        out_e, in_e = face(h_east, u, u_east)
        in_w, out_w = face(h_west, u_west, u)
        out_n, in_n = face(h_north, v, v_north)
        in_s, out_s = face(h_south, v_south, v)
        coef[0, k] = in_w
        coef[1, k] = in_e
        coef[2, k] = in_s
        coef[3, k] = in_n
        coef[4, k] = (out_e + out_w) + (out_n + out_s)
        coef[5, k] = grid_area * h

    def step(k, t):
        x = tracers[t, k]
        x_east, x_west = around(x, t, k)
        x_north, x_south = along(x, t, k)
        change = (coef[0, k] * x_west + coef[1, k] * x_east) + (
            coef[2, k] * x_south + coef[3, k] * x_north
        )
        new = x + (change - coef[4, k] * x)
        updated[t, k] = new
        product[t] = new * coef[5, k]

    def pooled(fields):
        upper, lower, whole = [], [], []
        for t in fields:
            both = []
            for i in range(quads):
                four = [
                    product[t, pl.ds(4 * i + j, bands, stride=BAND_ROWS), :] for j in range(4)
                ]
                upper.append(four[0] + four[1])
                lower.append(four[2] + four[3])
                both.append(upper[-1] + lower[-1])
            whole.append(jnp.concatenate(both, axis=1))
        halves = [jnp.concatenate(upper, axis=0), jnp.concatenate(lower, axis=0)]
        two = exact_dot(jnp.concatenate(halves, axis=1), pool_two[...])
        four = exact_dot(jnp.concatenate(whole, axis=0), pool_four[...])
        return two, four

    def rows_at(k, count):
        return pl.ds(pl.multiple_of(k * count, count), count)

    def keep(k, t, two, four):
        at_rows = rows_at(k, bands)
        ratio = two / den_two[rows_at(k, span), :]
        for i in range(quads):
            column = (t * quads + i) * nc
            blocks[at_rows, column : column + nc] = ratio[i * bands : (i + 1) * bands]
        column = (nt * quads + t) * nc
        blocks[at_rows, column : column + nc] = four / den_four[at_rows, :]

    def first(k, carry):
        faces(k)
        product[nt] = coef[5, k]
        step(k, 0)
        two, four = pooled((0, nt))
        den_two[rows_at(k, span), :] = jnp.maximum(two[span:], weight_floor)
        den_four[rows_at(k, bands), :] = jnp.maximum(four[bands:], weight_floor)
        keep(k, 0, two[:span], four[:bands])
        return carry

    def rest(k, carry):
        for t in range(1, nt):
            step(k, t)
        level_out(k).start()
        two, four = pooled(range(1, nt))
        for t in range(1, nt):
            keep(k, t, two[(t - 1) * span : t * span], four[(t - 1) * bands : t * bands])
        return carry

    def placed(send, start, width):
        for at in range(0, width, quads * nc):
            source = blocks[:, start + at : start + at + quads * nc]
            send[:, at : at + quads * nc] = dot(
                place[...], jnp.concatenate(pieces(source), axis=0)
            )

    part = quads * nc
    moves = (
        (send_first, two_out, 0, part),
        (send_rest, two_out, part, (nt - 1) * part),
        (send_four, four_out, 0, nt * nc),
    )
    mine = rows_at(me, rows_each)

    def transfer(index, j, peer, source_rows, target_rows):
        send, out, start, width = moves[index]
        return pltpu.make_async_remote_copy(
            src_ref=send.at[source_rows, :],
            dst_ref=out.at[target_rows, pl.ds(start, width)],
            send_sem=send_sem.at[index, j],
            recv_sem=recv_sem.at[index, j],
            device_id=(peer // n_lat, lax.rem(peer, n_lat)),
            device_id_type=MESH,
        )

    def to_peer(index, j):
        peer = lax.rem(me + j, n)
        return transfer(index, j, peer, rows_at(peer, rows_each), mine)

    def from_peer(index, j):
        peer = lax.rem(me + n - j, n)
        return transfer(index, j, peer, mine, rows_at(peer, rows_each))

    def own_copy(index):
        send, out, start, width = moves[index]
        return pltpu.make_async_copy(
            send.at[mine, :], out.at[mine, pl.ds(start, width)], send_sem.at[index, 0]
        )

    def begin(indices):
        def body(j, carry):
            for index in indices:
                to_peer(index, j).start()
            return carry

        lax.fori_loop(1, n, body, 0)
        for index in indices:
            own_copy(index).start()

    lax.fori_loop(0, nl, first, 0)
    placed(send_first, 0, part)
    begin((0,))
    lax.fori_loop(0, nl, rest, 0)
    placed(send_rest, part, (nt - 1) * part)
    placed(send_four, nt * part, nt * nc)
    begin((1, 2))

    def end_level(k, carry):
        level_out(k).wait()
        return carry

    lax.fori_loop(0, nl, end_level, 0)
    for index in range(3):
        own_copy(index).wait()

    def end(j, carry):
        for index in range(3):
            to_peer(index, j).wait_send()
            from_peer(index, j).wait_recv()
        return carry

    lax.fori_loop(1, n, end, 0)


def local(
    tracers, fill_fraction, ocean_mask, east_speed, north_speed, diffusivity, cell_area, owner_map
):
    nt, nl, nr, nc = tracers.shape
    n_lon = lax.axis_size("lon")
    n_lat = lax.axis_size("lat")
    n = n_lon * n_lat
    units = owner_map.shape[0]
    capacity = max(2, 2 * units // n)
    rows_each = -(-capacity // 8) * 8
    wide_two = nt * BAND_ROWS * nc // 4
    wide_four = nt * BAND_ROWS * nc // 16
    wide = wide_two + wide_four
    items = (nt + 2) * nl
    f32 = jnp.float32
    hbm = pl.BlockSpec(memory_space=pltpu.HBM)
    part = wide_two // nt
    updated, two, four = pl.pallas_call(
        functools.partial(kernel, (n_lon, n_lat, rows_each)),
        out_shape=(
            jax.ShapeDtypeStruct(tracers.shape, f32),
            jax.ShapeDtypeStruct((n * rows_each, wide_two), f32),
            jax.ShapeDtypeStruct((n * rows_each, wide_four), f32),
        ),
        in_specs=[hbm] * 5 + [pl.BlockSpec(memory_space=pltpu.SMEM)] + [hbm] * 2,
        out_specs=(hbm, hbm, hbm),
        scratch_shapes=[
            pltpu.VMEM(tracers.shape, f32),
            pltpu.VMEM((nl, nr, nc), f32),
            pltpu.VMEM((nl, nr, nc), jnp.int32),
            pltpu.VMEM((nl, nr, nc), f32),
            pltpu.VMEM((nl, nr, nc), f32),
            pltpu.VMEM((nr, nc), f32),
            pltpu.VMEM((1, units), jnp.int32),
            pltpu.VMEM(tracers.shape, f32),
            pltpu.VMEM((6, nl, nr, nc), f32),
            pltpu.VMEM((nt + 1, nr, nc), f32),
            pltpu.VMEM((units * BAND_ROWS // 4, nc), f32),
            pltpu.VMEM((units, nc), f32),
            pltpu.VMEM((units, wide), f32),
            pltpu.VMEM((n * rows_each, part), f32),
            pltpu.VMEM((n * rows_each, wide_two - part), f32),
            pltpu.VMEM((n * rows_each, wide_four), f32),
            pltpu.VMEM((n * rows_each, 3 * units), jnp.bfloat16),
            pltpu.VMEM((2 * nc, nc), jnp.bfloat16),
            pltpu.VMEM((4 * nc, nc), jnp.bfloat16),
            pltpu.VMEM((2, nr, nc), f32),
            pltpu.VMEM((2, nr, nc), f32),
            pltpu.VMEM((2, items, nc), f32),
            pltpu.VMEM((2, items, nc), f32),
            pltpu.SemaphoreType.DMA((4,)),
            pltpu.SemaphoreType.DMA((4,)),
            pltpu.SemaphoreType.DMA((3, n)),
            pltpu.SemaphoreType.DMA((3, n)),
            pltpu.SemaphoreType.DMA((nl,)),
            pltpu.SemaphoreType.DMA((7,)),
        ],
        compiler_params=pltpu.CompilerParams(
            collective_id=0, has_side_effects=True, vmem_limit_bytes=56 * 1024 * 1024
        ),
        name="substep",
    )(
        tracers,
        fill_fraction,
        ocean_mask,
        east_speed,
        north_speed,
        diffusivity,
        cell_area,
        owner_map.reshape(1, units),
    )
    if rows_each != capacity:
        two, four = (
            got.reshape(n, rows_each, -1)[:, :capacity].reshape(n * capacity, -1)
            for got in (two, four)
        )
    return updated, two[None], four[None]


def solution(mesh):
    in_specs = (
        P(None, None, "lat", "lon"),
        P(None, "lat", "lon"),
        P(None, "lat", "lon"),
        P(None, "lat", "lon"),
        P(None, "lat", "lon"),
        P(),
        P("lat", "lon"),
        P(("lon", "lat"), None),
    )
    out_specs = (
        P(None, None, "lat", "lon"),
        P(("lon", "lat"), None, None),
        P(("lon", "lat"), None, None),
    )
    return jax.shard_map(local, mesh=mesh, in_specs=in_specs, out_specs=out_specs, check_vma=False)
```
